512 devices in a mesh: row: 16 (over z_hi, x, core), col: 32 (over y, z_lo).
Axes of the slice: x: 4, y: 8, z: 8 (z_hi: 2, z_lo: 4; z = z_hi * 4 + z_lo), core: 2. Of those that a mesh axis runs over, the one named last changes fastest.
Arguments:
- residual: bfloat16 [32768, 1536], P(('row', 'col')), may hold values from -6 to 6
- bins: int32 [32768], P(('row', 'col')), may hold values from 0 to 15
- bin_scale: float32 [16], replicated, may hold values from 0.1 to 1
- blocks: bfloat16 [32768, 12288], P(('row', 'col')), may hold values from -0.4375 to 0.4375
- block_row: int32 [32768], P(('row', 'col')), may hold values from 0 to 2047, as said below
- block_col: int32 [32768], P(('row', 'col')), may hold values from 0 to 7
- counts: int32 [8192], P(('row', 'col')), may hold values from 1 to 4, as said below
Outputs:
- coarse: float32 [32, 128, 512], P('col', 'row')
The draws below stay inside these ranges and needn't reach their ends.
Inputs may be any that keep to these rules, and one draw needn't show every extreme that they name: `counts`: every device has a bucket with 4 live slots, and in one column group every row group sends 4 live slots to the same aggregate piece. Among the 16 * 4 slots of one device, at most 4 have the same value of block_row // 64, and exactly 4 for some value.
All inputs are finite; a program needn't handle non-finite values.
Results may differ from the reference program's by a relative error of at most 0.00035.
Values may be sent and summed in bfloat16 or wider, within the bound.
A program may use at most 64 MiB of HBM per device.

```python
import math
import jax
import jax.numpy as jnp
from jax import lax

BF = 192
BA = 64
CASES = 8
NBINS = 16
REQ = 4
FB_DEV = 64
CAP = 4
AG_DEV = 8
FINE = 32768
SLOTS = 32768
N_ROW = 16
N_COL = 32


def draw_counts(key, part):
    key = jax.random.fold_in(key, 11)
    first, second, third, fourth = jax.random.split(key, 4)
    groups = N_ROW * N_COL
    base = jax.random.randint(first, (groups, N_ROW), 1, CAP + 1)
    bucket = jnp.arange(N_ROW, dtype=jnp.int32)[None, :]
    full_one = jax.random.randint(second, (groups, 1), 0, N_ROW)
    base = jnp.where(bucket == full_one, CAP, base)
    hot_col = jax.random.randint(third, (), 0, N_COL)
    hot_dest = jax.random.randint(fourth, (), 0, N_ROW)
    column = (jnp.arange(groups, dtype=jnp.int32) % N_COL)[:, None]
    base = jnp.where((column == hot_col) & (bucket == hot_dest), CAP, base)
    return base.reshape(-1).astype(jnp.int32)


def draw_block_row(key, part):
    key = jax.random.fold_in(key, 23)
    slots_dev = N_ROW * CAP

    def one_device(device_key):
        first, second, third, fourth = jax.random.split(device_key, 4)
        hot_owner = jax.random.randint(first, (), 0, N_COL).astype(jnp.int32)
        others = jax.random.permutation(second, (N_COL - 1) * REQ)[:slots_dev - REQ].astype(jnp.int32)
        owner_rest = (others // REQ + hot_owner + 1) % N_COL
        owner = jnp.concatenate([jnp.full((REQ,), hot_owner, dtype=jnp.int32), owner_rest])
        owner = owner[jax.random.permutation(third, slots_dev)]
        local = jax.random.randint(fourth, (slots_dev,), 0, FB_DEV).astype(jnp.int32)
        return owner * FB_DEV + local
    device_keys = jax.random.split(key, N_ROW * N_COL)
    return jax.vmap(one_device)(device_keys).reshape(-1).astype(jnp.int32)


def place_ends(result, key, low, high):
    longest = result.shape.index(max(result.shape))
    spots = []
    for shift in (0, 1):
        where = [jax.random.randint(jax.random.fold_in(key, axis), (), 0, length) for axis, length in enumerate(result.shape)]
        where[longest] = (where[longest] + shift) % result.shape[longest]
        spots.append(tuple(where))
    return result.at[spots[0]].set(low).at[spots[1]].set(high)


def level_of(key, shape, cuts, low, high):
    loudness, own = 1.0, jax.random.fold_in(key, 6)
    for axis_at, shards_of in cuts:
        draws = jnp.exp(jax.random.uniform(jax.random.fold_in(own, axis_at), (shards_of,), jnp.float32, low / len(cuts), high / len(cuts)))
        loudness = loudness * jnp.repeat(draws, shape[axis_at] // shards_of).reshape([-1 if axis == axis_at else 1 for axis in range(len(shape))])
    return loudness


def scatter_about(rng, extent, spread, bound, pieces=(), kind=jnp.bfloat16):
    entries = spread * jax.random.normal(rng, extent, jnp.float32)
    if pieces:
        entries = entries * level_of(rng, extent, pieces, -0.22, 0.18)
    return jnp.clip(entries, -bound, bound).astype(kind)


def setup_inputs(seed: int = 0) -> dict:
    splits = jax.random.split(jax.random.key(seed), 8)
    return {
        "residual": scatter_about(splits[0], (FINE, CASES * BF), 1.0, 6.0, ((0, 512),)),
        "bins": place_ends(jax.random.randint(splits[1], (FINE,), 0, NBINS), jax.random.fold_in(splits[1], 1), 0, NBINS - 1).astype(jnp.int32),
        "bin_scale": jnp.clip(jnp.exp(jax.random.uniform(splits[2], (NBINS,), jnp.float32, math.log(0.1), math.log(1.0))), 0.1, 1.0),
        "blocks": scatter_about(splits[3], (SLOTS, BF * BA), BF ** -0.5, 0.4375, ((0, 512),)),
        "block_row": draw_block_row(jax.random.fold_in(splits[7], 71), 0),
        "block_col": place_ends(jax.random.randint(splits[5], (SLOTS,), 0, AG_DEV), jax.random.fold_in(splits[5], 1), 0, AG_DEV - 1).astype(jnp.int32),
        "counts": draw_counts(jax.random.fold_in(splits[7], 71), 0),
    }


def reference(residual, bins, bin_scale, blocks, block_row, block_col, counts):
    slots_dev = N_ROW * CAP
    devices = N_ROW * N_COL
    slot = jnp.arange(devices * slots_dev, dtype=jnp.int32)
    device = slot // slots_dev
    row_group = device // N_COL
    col_group = device % N_COL
    dest = (slot // CAP) % N_ROW
    place = slot % CAP
    fine = row_group * (FB_DEV * N_COL) + block_row
    live = (place < counts[device * N_ROW + dest]).astype(jnp.float32)
    weight = bin_scale[bins[fine]] * live
    target = col_group * (AG_DEV * N_ROW) + dest * AG_DEV + block_col
    picked = residual[fine].reshape(devices, slots_dev, CASES, BF)
    shaped = blocks.reshape(devices, slots_dev, BF * BA)

    def one_device(pair):
        panel, block = pair
        panel = panel.astype(jnp.float32)
        block = block.reshape(slots_dev, BF, BA).astype(jnp.float32)
        prod = jnp.einsum('scf,sfa->sca', panel, block)
        return prod.reshape(slots_dev, CASES * BA)

    terms = lax.map(one_device, (picked, shaped)).reshape(-1, CASES * BA)
    terms = weight[:, None] * terms
    coarse = jax.ops.segment_sum(terms, target, num_segments=N_COL * AG_DEV * N_ROW)
    return coarse.reshape(N_COL, AG_DEV * N_ROW, CASES * BA)
```

```python
import functools

import jax
import jax.numpy as jnp
from jax import lax
from jax.experimental import pallas as pl
from jax.experimental.pallas import tpu as pltpu
from jax.sharding import PartitionSpec as P

CASES = 8
AG_DEV = 8
REQ = 4
LANES = 128
MESH = pl.DeviceIdType.MESH


def iota(shape, dim):
    return lax.broadcasted_iota(jnp.int32, shape, dim)


def dot(a, b, dims=((1,), (0,))):
    return lax.dot_general(
        a.astype(jnp.bfloat16),
        b.astype(jnp.bfloat16),
        (dims, ((), ())),
        preferred_element_type=jnp.float32,
    )


def wait_bytes(ref, sem):
    pltpu.make_async_copy(ref, ref, sem).wait()


def pair_up(row, pairs):
    shape = (pairs, row.shape[1])
    spread = jnp.broadcast_to(row, shape)
    low = jnp.sum(jnp.where(iota(shape, 1) == 2 * iota(shape, 0), spread, 0.0), axis=1, keepdims=True)
    high = jnp.sum(jnp.where(iota(shape, 1) == 2 * iota(shape, 0) + 1, spread, 0.0), axis=1, keepdims=True)
    wide = (pairs, LANES)
    return jnp.where(iota(wide, 1) < LANES // 2, jnp.broadcast_to(low, wide), jnp.broadcast_to(high, wide))


def kernel(
    n_row,
    n_col,
    residual,
    blocks,
    block_row_at,
    block_col_at,
    bins_at,
    counts_at,
    bin_scale_at,
    coarse,
    block_row,
    block_col,
    bins,
    counts,
    bin_scale,
    padded,
    res,
    blk,
    wide,
    packed,
    table,
    ask,
    asked,
    asked_s,
    place,
    place_s,
    answer,
    got,
    terms,
    summands,
    cols,
    got_cols,
    weights,
    folded,
    load_sem,
    place_sem,
    ask_sem,
    ask_in,
    asked_sem,
    answer_sem,
    answer_in,
    term_sem,
    term_in,
    cols_sem,
    cols_in,
):
    row, col = lax.axis_index("row"), lax.axis_index("col")
    fine_dev, width = res.shape
    slots = blk.shape[0]
    cap = slots // n_row
    dofs = width // CASES
    half = dofs // 2
    groups = 2 * CASES
    tiles = blk.shape[1] // LANES

    small = [
        pltpu.make_async_copy(a, b, load_sem.at[2 + i])
        for i, (a, b) in enumerate(
            (
                (block_row_at, block_row),
                (block_col_at, block_col),
                (bins_at, bins),
                (counts_at, counts),
                (bin_scale_at, bin_scale),
            )
        )
    ]
    for load in small:
        load.start()
    load_res = pltpu.make_async_copy(residual, res, load_sem.at[0])
    load_res.start()
    load_blk = pltpu.make_async_copy(blocks, blk, load_sem.at[1])
    load_blk.start()

    barrier = pltpu.get_barrier_semaphore()

    @pl.loop(1, n_col)
    def _(j):
        pl.semaphore_signal(barrier, inc=1, device_id={"col": lax.rem(col + j, n_col)}, device_id_type=MESH)

    @pl.loop(1, n_row)
    def _(j):
        pl.semaphore_signal(barrier, inc=1, device_id={"row": lax.rem(row + j, n_row)}, device_id_type=MESH)

    for load in small:
        load.wait()

    rows = block_row[...]
    owner = lax.div(rows, fine_dev)
    local = lax.rem(rows, fine_dev)
    square = (slots, slots)
    down, across = iota(square, 0), iota(square, 1)
    owner_down = jnp.sum(
        jnp.where(down == across, jnp.broadcast_to(owner, square), 0), axis=1, keepdims=True
    )
    rank = jnp.sum(jnp.where((owner_down == owner) & (down < across), 1, 0), axis=0, keepdims=True)
    owned = owner == iota((n_col, slots), 0)
    lane = iota((n_col, LANES), 1)
    padded[...] = jnp.zeros_like(padded)
    padded[:, 0:fine_dev] = bins[...]
    message = jnp.broadcast_to(padded[...], (n_col, LANES))
    for k in range(REQ):
        wanted = jnp.sum(jnp.where(owned & (rank == k), local, 0), axis=1, keepdims=True)
        message = jnp.where(lane == fine_dev + k, wanted, message)
    for c in range(n_col):
        ask[c] = message[c : c + 1, :]

    place[:, 0:slots] = owner * REQ + rank
    store_place = pltpu.make_async_copy(place, place_s, place_sem)
    store_place.start()

    paired = pair_up(block_col[...].astype(jnp.float32), slots // 2).astype(jnp.int32)
    for d in range(n_row):
        cols[d] = paired[d * cap // 2 : (d + 1) * cap // 2, :]

    lane = iota((1, 4 * LANES), 1)
    within = lax.rem(lane, LANES)
    group = lax.div(lane, LANES)
    source = jnp.where(within < half, lax.div(group, 2) * dofs + 2 * within + lax.rem(group, 2), -1)
    spread = (iota((2 * dofs, 4 * LANES), 0) == source).astype(jnp.bfloat16)
    load_res.wait()
    for q in range(CASES // 2):
        two = dot(res[:, 2 * dofs * q : 2 * dofs * (q + 1)], spread)
        for g in range(4):
            at = (g % 2) * CASES + 2 * q + g // 2
            wide[pl.ds(at, fine_dev, stride=groups), :] = two[:, g * LANES : (g + 1) * LANES]
    table[...] = wide[0 : fine_dev * groups, :].reshape(fine_dev, groups, LANES)

    pl.semaphore_wait(barrier, n_col + n_row - 2)

    def to_col(src, dst, send, recv, peer):
        return pltpu.make_async_remote_copy(
            src_ref=src, dst_ref=dst, send_sem=send, recv_sem=recv, device_id={"col": peer}, device_id_type=MESH
        )

    def to_row(src, dst, send, recv, peer):
        return pltpu.make_async_remote_copy(
            src_ref=src, dst_ref=dst, send_sem=send, recv_sem=recv, device_id={"row": peer}, device_id_type=MESH
        )

    @pl.loop(1, n_col)
    def _(j):
        peer = lax.rem(col + j, n_col)
        to_col(ask.at[peer], asked.at[col], ask_sem, ask_in, peer).start()

    asked[col] = ask[col]

    @pl.loop(1, n_row)
    def _(j):
        peer = lax.rem(row + j, n_row)
        to_row(cols.at[peer], got_cols.at[row], cols_sem, cols_in, peer).start()

    got_cols[row] = cols[row]

    wait_bytes(ask.at[pl.ds(0, n_col - 1)], ask_in)
    to_smem = pltpu.make_async_copy(asked, asked_s, asked_sem)
    to_smem.start()
    to_smem.wait()

    thirds = LANES - half
    low_lanes = iota((groups, LANES), 1) < half

    def rows_for(peer):
        picked = []
        for k in range(REQ):
            picked.append(table[asked_s[peer, 0, fine_dev + k]])
        return [
            jnp.where(low_lanes, picked[v], pltpu.roll(picked[3], half - thirds * v, 1)).astype(jnp.bfloat16)
            for v in range(3)
        ]

    @pl.loop(1, n_col)
    def _(j):
        peer = lax.rem(col + j, n_col)
        for v, tile in enumerate(rows_for(peer)):
            answer[peer, v] = tile
        to_col(answer.at[peer], got.at[pl.ds(col * REQ, 3)], answer_sem, answer_in, peer).start()

    for v, tile in enumerate(rows_for(col)):
        got[col * REQ + v] = tile

    load_blk.wait()

    @pl.loop(0, tiles, unroll=4)
    def _(t):
        at = pl.multiple_of(t * LANES, LANES)
        wide[pl.ds(t, slots, stride=tiles), :] = blk[:, pl.ds(at, LANES)].astype(jnp.float32)

    @pl.loop(0, slots)
    def _(s):
        at = pl.multiple_of(s * tiles, 8)
        packed[s, 0:half, :] = wide[pl.ds(at, half), :].astype(jnp.bfloat16)
        packed[s, half:, :] = jnp.zeros((LANES - half, LANES), jnp.bfloat16)

    all_bins = asked[...].reshape(n_col, LANES).astype(jnp.float32)
    here = (local == iota((LANES, slots), 0)).astype(jnp.float32)
    bin_of = jnp.sum(jnp.where(owned, dot(all_bins, here), 0.0), axis=0, keepdims=True).astype(jnp.int32)
    n_bins = bin_scale.shape[1]
    square = (n_bins, n_bins)
    scales = jnp.sum(
        jnp.where(iota(square, 0) == iota(square, 1), jnp.broadcast_to(bin_scale[...], square), 0.0),
        axis=1,
        keepdims=True,
    )
    scale_of = jnp.sum(jnp.where(bin_of == iota((n_bins, slots), 0), scales, 0.0), axis=0, keepdims=True)
    of_bucket = (lax.div(iota((n_row, slots), 1), cap) == iota((n_row, slots), 0)).astype(jnp.float32)
    live = lax.rem(iota((1, slots), 1), cap).astype(jnp.float32) < dot(counts[...].astype(jnp.float32), of_bucket)
    weights[...] = pair_up(jnp.where(live, scale_of, 0.0), slots // 2)

    store_place.wait()
    wait_bytes(answer.at[pl.ds(0, n_col - 1)], answer_in)

    lane_at = iota((groups, LANES), 1)

    @pl.loop(0, n_col)
    def _(c):
        a, b, d = (
            pltpu.roll(got[c * REQ + v].astype(jnp.float32), thirds * (v + 1), 1) for v in range(3)
        )
        got[c * REQ + 3] = jnp.where(
            lane_at < thirds, a, jnp.where(lane_at < 2 * thirds, b, d)
        ).astype(jnp.bfloat16)

    low = iota((CASES, LANES), 1) < LANES // 2

    def term(slot):
        panel = got[place_s[0, slot]]
        both = jnp.dot(panel, packed[slot], preferred_element_type=jnp.float32)
        return both[:CASES], both[CASES:]

    def bucket(d, dest, at):
        for pair in range(cap // 2):
            a0, a1 = term(d * cap + 2 * pair)
            b0, b1 = term(d * cap + 2 * pair + 1)
            both = jnp.where(low, a0, b1) + pltpu.roll(jnp.where(low, b0, a1), LANES // 2, 1)
            weight = weights[pl.ds(d * (cap // 2) + pair, 1), :]
            dest[at, pair * CASES : (pair + 1) * CASES, :] = both * weight

    @pl.loop(1, n_row)
    def _(j):
        peer = lax.rem(row + j, n_row)
        bucket(peer, terms, peer)
        to_row(terms.at[peer], summands.at[row], term_sem, term_in, peer).start()

    bucket(row, summands, row)

    wait_bytes(cols.at[pl.ds(0, n_row - 1)], cols_in)
    wait_bytes(terms.at[pl.ds(0, n_row - 1)], term_in)

    def add(r, sums):
        for pair in range(cap // 2):
            value = summands[r, pair * CASES : (pair + 1) * CASES, :]
            to = got_cols[r, pair : pair + 1, :]
            sums = tuple(s + jnp.where(to == a, value, 0.0) for a, s in enumerate(sums))
        return sums

    sums = lax.fori_loop(0, n_row, add, (jnp.zeros((CASES, LANES), jnp.float32),) * AG_DEV)
    for a, s in enumerate(sums):
        s = s + pltpu.roll(s, LANES // 2, 1)
        folded[a * CASES : (a + 1) * CASES, :] = jnp.where(low, s, pltpu.roll(s, CASES - 1, 0))
    for j in range(CASES // 2):
        coarse[:, j * LANES : (j + 1) * LANES] = folded[pl.ds(2 * j, AG_DEV, stride=CASES), :]

    wait_bytes(ask.at[pl.ds(0, n_col - 1)], ask_sem)
    wait_bytes(cols.at[pl.ds(0, n_row - 1)], cols_sem)
    wait_bytes(answer.at[pl.ds(0, n_col - 1)], answer_sem)
    wait_bytes(terms.at[pl.ds(0, n_row - 1)], term_sem)


def shards(n_row, n_col, residual, bins, bin_scale, blocks, block_row, block_col, counts):
    slots, entries = blocks.shape
    fine_dev, width = residual.shape
    cap = slots // n_row
    dofs = width // CASES
    aggregate = entries // dofs
    tiles = entries // LANES
    f32, bf16, i32 = jnp.float32, jnp.bfloat16, jnp.int32
    vmem = pl.BlockSpec(memory_space=pltpu.VMEM)
    hbm = pl.BlockSpec(memory_space=pltpu.HBM)
    dma = pltpu.SemaphoreType.DMA
    out = pl.pallas_call(
        functools.partial(kernel, n_row, n_col),
        out_shape=jax.ShapeDtypeStruct((AG_DEV, CASES * aggregate), f32),
        in_specs=[hbm] * 7,
        out_specs=vmem,
        scratch_shapes=[
            pltpu.VMEM((1, slots), i32),
            pltpu.VMEM((1, slots), i32),
            pltpu.VMEM((1, fine_dev), i32),
            pltpu.VMEM((1, n_row), i32),
            pltpu.VMEM((1, bin_scale.shape[0]), f32),
            pltpu.VMEM((1, LANES), i32),
            pltpu.VMEM((fine_dev, width), bf16),
            pltpu.VMEM((slots, entries), bf16),
            pltpu.VMEM((slots * tiles, LANES), f32),
            pltpu.VMEM((slots, LANES, LANES), bf16),
            pltpu.VMEM((fine_dev, 2 * CASES, LANES), f32),
            pltpu.VMEM((n_col, 1, LANES), i32),
            pltpu.VMEM((n_col, 1, LANES), i32),
            pltpu.SMEM((n_col, 1, LANES), i32),
            pltpu.VMEM((1, LANES), i32),
            pltpu.SMEM((1, LANES), i32),
            pltpu.VMEM((n_col, 3, 2 * CASES, LANES), bf16),
            pltpu.VMEM((n_col * REQ, 2 * CASES, LANES), bf16),
            pltpu.VMEM((n_row, cap // 2 * CASES, LANES), f32),
            pltpu.VMEM((n_row, cap // 2 * CASES, LANES), f32),
            pltpu.VMEM((n_row, cap // 2, LANES), i32),
            pltpu.VMEM((n_row, cap // 2, LANES), i32),
            pltpu.VMEM((slots // 2, LANES), f32),
            pltpu.VMEM((AG_DEV * CASES, LANES), f32),
            dma((7,)),
        ]
        + [dma] * 10,
        compiler_params=pltpu.CompilerParams(
            collective_id=0, has_side_effects=True, vmem_limit_bytes=60 * 1024 * 1024
        ),
    )(
        residual,
        blocks,
        block_row.reshape(1, -1),
        block_col.reshape(1, -1),
        bins.reshape(1, -1),
        counts.reshape(1, -1),
        bin_scale.reshape(1, -1),
    )
    return out[None]


def solution(mesh):
    both = P(("row", "col"))
    rows = P(("row", "col"), None)
    return jax.shard_map(
        functools.partial(shards, mesh.shape["row"], mesh.shape["col"]),
        mesh=mesh,
        in_specs=(rows, both, P(), rows, both, both, both),
        out_specs=P("col", "row", None),
        check_vma=False,
    )
```

```python
import functools

import jax
import jax.numpy as jnp
from jax import lax
from jax.experimental import pallas as pl
from jax.experimental.pallas import tpu as pltpu
from jax.sharding import PartitionSpec as P

CASES = 8
AG_DEV = 8
REQ = 4
LANES = 128
RUN = 4
MESH = pl.DeviceIdType.MESH


def iota(shape, dim):
    return lax.broadcasted_iota(jnp.int32, shape, dim)


def dot(a, b, dims=((1,), (0,))):
    return lax.dot_general(
        a.astype(jnp.bfloat16),
        b.astype(jnp.bfloat16),
        (dims, ((), ())),
        preferred_element_type=jnp.float32,
    )


def wait_bytes(ref, sem):
    pltpu.make_async_copy(ref, ref, sem).wait()


def pair_up(row, pairs):
    shape = (pairs, row.shape[1])
    spread = jnp.broadcast_to(row, shape)
    low = jnp.sum(jnp.where(iota(shape, 1) == 2 * iota(shape, 0), spread, 0.0), axis=1, keepdims=True)
    high = jnp.sum(jnp.where(iota(shape, 1) == 2 * iota(shape, 0) + 1, spread, 0.0), axis=1, keepdims=True)
    wide = (pairs, LANES)
    return jnp.where(iota(wide, 1) < LANES // 2, jnp.broadcast_to(low, wide), jnp.broadcast_to(high, wide))


def kernel(
    n_row,
    n_col,
    residual,
    blocks,
    block_row_at,
    block_col_at,
    bins_at,
    counts_at,
    bin_scale_at,
    coarse,
    block_row,
    block_col,
    bins,
    counts,
    bin_scale,
    padded,
    res,
    blk,
    wide,
    packed,
    table,
    ask,
    asked,
    asked_s,
    place,
    place_s,
    answer,
    got,
    terms,
    summands,
    cols,
    got_cols,
    weights,
    folded,
    load_sem,
    place_sem,
    ask_sem,
    ask_in,
    asked_sem,
    answer_sem,
    answer_in,
    term_sem,
    term_in,
    cols_sem,
    cols_in,
):
    row, col = lax.axis_index("row"), lax.axis_index("col")
    fine_dev, width = res.shape
    slots = blk.shape[0]
    cap = slots // n_row
    dofs = width // CASES
    half = dofs // 2
    groups = 2 * CASES
    tiles = blk.shape[1] // LANES

    n_z = min(RUN, n_col)
    n_y = n_col // n_z

    def col_peer(group, i):
        far = n_y - 1 - group
        step = lax.div(far + 1, 2) * (2 * lax.rem(far, 2) - 1)
        y = lax.rem(lax.div(col, n_z) + n_y // 2 + step + n_y, n_y)
        return y * n_z + lax.rem(lax.rem(col, n_z) + i + 1, n_z)

    halves = n_row // 2

    def row_peer(t):
        near = lax.div(t, halves)
        half_of = lax.rem(lax.div(row, halves) + 1 - near, 2)
        return half_of * halves + lax.rem(lax.rem(row, halves) + lax.rem(t, halves) + near, halves)

    barrier = pltpu.get_barrier_semaphore()

    def greet_col(group, i):
        pl.semaphore_signal(barrier, inc=1, device_id={"col": col_peer(group, i)}, device_id_type=MESH)

    @pl.loop(0, n_y - 1)
    def _(g):
        for i in range(n_z):
            greet_col(n_y - 1 - g, i)

    @pl.loop(0, n_row - 1)
    def _(t):
        pl.semaphore_signal(barrier, inc=1, device_id={"row": row_peer(t)}, device_id_type=MESH)

    for i in range(n_z - 1):
        greet_col(0, i)

    small = [
        pltpu.make_async_copy(a, b, load_sem.at[2 + i])
        for i, (a, b) in enumerate(
            (
                (block_row_at, block_row),
                (block_col_at, block_col),
                (bins_at, bins),
                (counts_at, counts),
                (bin_scale_at, bin_scale),
            )
        )
    ]
    for load in small:
        load.start()
    load_res = pltpu.make_async_copy(residual, res, load_sem.at[0])
    load_res.start()
    load_blk = pltpu.make_async_copy(blocks, blk, load_sem.at[1])
    load_blk.start()
    for load in small:
        load.wait()

    rows = block_row[...]
    owner = lax.div(rows, fine_dev)
    local = lax.rem(rows, fine_dev)
    square = (slots, slots)
    down, across = iota(square, 0), iota(square, 1)
    owner_down = jnp.sum(
        jnp.where(down == across, jnp.broadcast_to(owner, square), 0), axis=1, keepdims=True
    )
    rank = jnp.sum(jnp.where((owner_down == owner) & (down < across), 1, 0), axis=0, keepdims=True)
    owned = owner == iota((n_col, slots), 0)
    lane = iota((n_col, LANES), 1)
    padded[...] = jnp.zeros_like(padded)
    padded[:, 0:fine_dev] = bins[...]
    message = jnp.broadcast_to(padded[...], (n_col, LANES))
    for k in range(REQ):
        wanted = jnp.sum(jnp.where(owned & (rank == k), local, 0), axis=1, keepdims=True)
        message = jnp.where(lane == fine_dev + k, wanted, message)
    for c in range(n_col):
        ask[c] = message[c : c + 1, :]

    place[:, 0:slots] = owner * REQ + rank
    store_place = pltpu.make_async_copy(place, place_s, place_sem)
    store_place.start()

    paired = pair_up(block_col[...].astype(jnp.float32), slots // 2).astype(jnp.int32)
    for d in range(n_row):
        cols[d] = paired[d * cap // 2 : (d + 1) * cap // 2, :]

    lane = iota((1, 4 * LANES), 1)
    within = lax.rem(lane, LANES)
    group = lax.div(lane, LANES)
    source = jnp.where(within < half, lax.div(group, 2) * dofs + 2 * within + lax.rem(group, 2), -1)
    spread = (iota((2 * dofs, 4 * LANES), 0) == source).astype(jnp.bfloat16)
    load_res.wait()
    for q in range(CASES // 2):
        two = dot(res[:, 2 * dofs * q : 2 * dofs * (q + 1)], spread)
        for g in range(4):
            at = (g % 2) * CASES + 2 * q + g // 2
            wide[pl.ds(at, fine_dev, stride=groups), :] = two[:, g * LANES : (g + 1) * LANES]
    table[...] = wide[0 : fine_dev * groups, :].reshape(fine_dev, groups, LANES)

    pl.semaphore_wait(barrier, n_col + n_row - 2)

    def to_col(src, dst, send, recv, peer):
        return pltpu.make_async_remote_copy(
            src_ref=src, dst_ref=dst, send_sem=send, recv_sem=recv, device_id={"col": peer}, device_id_type=MESH
        )

    def to_row(src, dst, send, recv, peer):
        return pltpu.make_async_remote_copy(
            src_ref=src, dst_ref=dst, send_sem=send, recv_sem=recv, device_id={"row": peer}, device_id_type=MESH
        )

    def request(group, i):
        peer = col_peer(group, i)
        to_col(ask.at[peer], asked.at[col], ask_sem, ask_in.at[col], peer).start()

    @pl.loop(0, n_y - 1)
    def _(g):
        for i in range(n_z):
            request(n_y - 1 - g, i)

    for i in range(n_z - 1):
        request(0, i)

    asked[col] = ask[col]

    @pl.loop(0, n_row - 1)
    def _(t):
        peer = row_peer(t)
        to_row(cols.at[peer], got_cols.at[row], cols_sem, cols_in.at[row], peer).start()

    got_cols[row] = cols[row]

    load_blk.wait()

    @pl.loop(0, tiles, unroll=4)
    def _(t):
        at = pl.multiple_of(t * LANES, LANES)
        wide[pl.ds(t, slots, stride=tiles), :] = blk[:, pl.ds(at, LANES)].astype(jnp.float32)

    @pl.loop(0, slots)
    def _(s):
        at = pl.multiple_of(s * tiles, 8)
        packed[s, 0:half, :] = wide[pl.ds(at, half), :].astype(jnp.bfloat16)
        packed[s, half:, :] = jnp.zeros((LANES - half, LANES), jnp.bfloat16)

    thirds = LANES - half
    low_lanes = iota((groups, LANES), 1) < half

    def rows_for(peer):
        picked = []
        for k in range(REQ):
            picked.append(table[asked_s[peer, 0, fine_dev + k]])
        return [
            jnp.where(low_lanes, picked[v], pltpu.roll(picked[3], half - thirds * v, 1)).astype(jnp.bfloat16)
            for v in range(3)
        ]

    def take(group, count):
        peers = [col_peer(group, i) for i in range(n_z)]
        for peer in peers[:count]:
            wait_bytes(asked.at[peer], ask_in.at[peer])
        for peer in peers:
            pltpu.make_async_copy(asked.at[peer], asked_s.at[peer], asked_sem.at[peer]).start()

    def reply(group, count):
        peers = [col_peer(group, i) for i in range(n_z)]
        for peer in peers:
            pltpu.make_async_copy(asked.at[peer], asked_s.at[peer], asked_sem.at[peer]).wait()
        filled = [rows_for(peer) for peer in peers]
        for peer, rows_of in zip(peers[:count], filled):
            for v, tile in enumerate(rows_of):
                answer[peer, v] = tile
            to_col(
                answer.at[peer], got.at[pl.ds(col * REQ, 3)], answer_sem, answer_in.at[col], peer
            ).start()
        if count < n_z:
            for v, tile in enumerate(filled[-1]):
                got[col * REQ + v] = tile

    take(0, n_z - 1)
    if n_y > 1:
        take(1, n_z)
    reply(0, n_z - 1)

    @pl.loop(2, n_y)
    def _(g):
        take(g, n_z)
        reply(g - 1, n_z)

    if n_y > 1:
        reply(n_y - 1, n_z)

    all_bins = asked[...].reshape(n_col, LANES).astype(jnp.float32)
    here = (local == iota((LANES, slots), 0)).astype(jnp.float32)
    bin_of = jnp.sum(jnp.where(owned, dot(all_bins, here), 0.0), axis=0, keepdims=True).astype(jnp.int32)
    n_bins = bin_scale.shape[1]
    square = (n_bins, n_bins)
    scales = jnp.sum(
        jnp.where(iota(square, 0) == iota(square, 1), jnp.broadcast_to(bin_scale[...], square), 0.0),
        axis=1,
        keepdims=True,
    )
    scale_of = jnp.sum(jnp.where(bin_of == iota((n_bins, slots), 0), scales, 0.0), axis=0, keepdims=True)
    of_bucket = (lax.div(iota((n_row, slots), 1), cap) == iota((n_row, slots), 0)).astype(jnp.float32)
    live = lax.rem(iota((1, slots), 1), cap).astype(jnp.float32) < dot(counts[...].astype(jnp.float32), of_bucket)
    weights[...] = pair_up(jnp.where(live, scale_of, 0.0), slots // 2)

    store_place.wait()
    lane_at = iota((groups, LANES), 1)

    def gather_thirds(group, count):
        peers = [col_peer(group, i) for i in range(n_z)]
        for peer in peers[:count]:
            wait_bytes(got.at[pl.ds(peer * REQ, 3)], answer_in.at[peer])
        joined = []
        for peer in peers:
            a, b, d = (
                pltpu.roll(got[peer * REQ + v].astype(jnp.float32), thirds * (v + 1), 1) for v in range(3)
            )
            joined.append(jnp.where(lane_at < thirds, a, jnp.where(lane_at < 2 * thirds, b, d)))
        for peer, tile in zip(peers, joined):
            got[peer * REQ + 3] = tile.astype(jnp.bfloat16)

    gather_thirds(0, n_z - 1)

    @pl.loop(1, n_y)
    def _(g):
        gather_thirds(g, n_z)

    low = iota((CASES, LANES), 1) < LANES // 2

    def term(slot):
        panel = got[place_s[0, slot]]
        both = jnp.dot(panel, packed[slot], preferred_element_type=jnp.float32)
        return both[:CASES], both[CASES:]

    def bucket(d):
        pairs = []
        for pair in range(cap // 2):
            a0, a1 = term(d * cap + 2 * pair)
            b0, b1 = term(d * cap + 2 * pair + 1)
            both = jnp.where(low, a0, b1) + pltpu.roll(jnp.where(low, b0, a1), LANES // 2, 1)
            pairs.append(both * weights[pl.ds(d * (cap // 2) + pair, 1), :])
        return pairs

    def store(dest, at, pairs):
        for pair, value in enumerate(pairs):
            dest[at, pair * CASES : (pair + 1) * CASES, :] = value

    def send(peers, summed):
        for peer, pairs in zip(peers, summed):
            store(terms, peer, pairs)
            to_row(terms.at[peer], summands.at[row], term_sem, term_in.at[row], peer).start()

    together = min(4, n_row)

    @pl.loop(0, n_row // together - 1)
    def _(g):
        peers = [row_peer(g * together + i) for i in range(together)]
        send(peers, [bucket(d) for d in peers])

    peers = [row_peer(n_row - together + i) for i in range(together - 1)]
    summed = [bucket(d) for d in peers + [row]]
    send(peers, summed[:-1])
    store(summands, row, summed[-1])

    def add(r, sums):
        for pair in range(cap // 2):
            value = summands[r, pair * CASES : (pair + 1) * CASES, :]
            to = got_cols[r, pair : pair + 1, :]
            sums = tuple(s + jnp.where(to == a, value, 0.0) for a, s in enumerate(sums))
        return sums

    def arrive(t, sums):
        peer = row_peer(n_row - 2 - t)
        wait_bytes(got_cols.at[peer], cols_in.at[peer])
        wait_bytes(summands.at[peer], term_in.at[peer])
        return add(peer, sums)

    sums = add(row, (jnp.zeros((CASES, LANES), jnp.float32),) * AG_DEV)
    sums = lax.fori_loop(0, n_row - 1, arrive, sums)
    for a, s in enumerate(sums):
        s = s + pltpu.roll(s, LANES // 2, 1)
        folded[a * CASES : (a + 1) * CASES, :] = jnp.where(low, s, pltpu.roll(s, CASES - 1, 0))
    for j in range(CASES // 2):
        coarse[:, j * LANES : (j + 1) * LANES] = folded[pl.ds(2 * j, AG_DEV, stride=CASES), :]

    wait_bytes(ask.at[pl.ds(0, n_col - 1)], ask_sem)
    wait_bytes(cols.at[pl.ds(0, n_row - 1)], cols_sem)
    wait_bytes(answer.at[pl.ds(0, n_col - 1)], answer_sem)
    wait_bytes(terms.at[pl.ds(0, n_row - 1)], term_sem)


def shards(n_row, n_col, residual, bins, bin_scale, blocks, block_row, block_col, counts):
    slots, entries = blocks.shape
    fine_dev, width = residual.shape
    cap = slots // n_row
    dofs = width // CASES
    aggregate = entries // dofs
    tiles = entries // LANES
    f32, bf16, i32 = jnp.float32, jnp.bfloat16, jnp.int32
    vmem = pl.BlockSpec(memory_space=pltpu.VMEM)
    hbm = pl.BlockSpec(memory_space=pltpu.HBM)
    dma = pltpu.SemaphoreType.DMA
    out = pl.pallas_call(
        functools.partial(kernel, n_row, n_col),
        out_shape=jax.ShapeDtypeStruct((AG_DEV, CASES * aggregate), f32),
        in_specs=[hbm] * 7,
        out_specs=vmem,
        scratch_shapes=[
            pltpu.VMEM((1, slots), i32),
            pltpu.VMEM((1, slots), i32),
            pltpu.VMEM((1, fine_dev), i32),
            pltpu.VMEM((1, n_row), i32),
            pltpu.VMEM((1, bin_scale.shape[0]), f32),
            pltpu.VMEM((1, LANES), i32),
            pltpu.VMEM((fine_dev, width), bf16),
            pltpu.VMEM((slots, entries), bf16),
            pltpu.VMEM((slots * tiles, LANES), f32),
            pltpu.VMEM((slots, LANES, LANES), bf16),
            pltpu.VMEM((fine_dev, 2 * CASES, LANES), f32),
            pltpu.VMEM((n_col, 1, LANES), i32),
            pltpu.VMEM((n_col, 1, LANES), i32),
            pltpu.SMEM((n_col, 1, LANES), i32),
            pltpu.VMEM((1, LANES), i32),
            pltpu.SMEM((1, LANES), i32),
            pltpu.VMEM((n_col, 3, 2 * CASES, LANES), bf16),
            pltpu.VMEM((n_col * REQ, 2 * CASES, LANES), bf16),
            pltpu.VMEM((n_row, cap // 2 * CASES, LANES), f32),
            pltpu.VMEM((n_row, cap // 2 * CASES, LANES), f32),
            pltpu.VMEM((n_row, cap // 2, LANES), i32),
            pltpu.VMEM((n_row, cap // 2, LANES), i32),
            pltpu.VMEM((slots // 2, LANES), f32),
            pltpu.VMEM((AG_DEV * CASES, LANES), f32),
            dma((7,)),
        ]
        + [dma, dma, dma((n_col,)), dma((n_col,)), dma, dma((n_col,))]
        + [dma, dma((n_row,)), dma, dma((n_row,))],
        compiler_params=pltpu.CompilerParams(
            collective_id=0, has_side_effects=True, vmem_limit_bytes=60 * 1024 * 1024
        ),
    )(
        residual,
        blocks,
        block_row.reshape(1, -1),
        block_col.reshape(1, -1),
        bins.reshape(1, -1),
        counts.reshape(1, -1),
        bin_scale.reshape(1, -1),
    )
    return out[None]


def solution(mesh):
    both = P(("row", "col"))
    rows = P(("row", "col"), None)
    return jax.shard_map(
        functools.partial(shards, mesh.shape["row"], mesh.shape["col"]),
        mesh=mesh,
        in_specs=(rows, both, P(), rows, both, both, both),
        out_specs=P("col", "row", None),
        check_vma=False,
    )
```

```python
import functools

import jax
import jax.numpy as jnp
from jax import lax
from jax.experimental import pallas as pl
from jax.experimental.pallas import tpu as pltpu
from jax.sharding import PartitionSpec as P

CASES = 8
AG_DEV = 8
REQ = 4
LANES = 128
RUN = 4
MESH = pl.DeviceIdType.MESH


def iota(shape, dim):
    return lax.broadcasted_iota(jnp.int32, shape, dim)


def dot(a, b, dims=((1,), (0,))):
    return lax.dot_general(
        a.astype(jnp.bfloat16),
        b.astype(jnp.bfloat16),
        (dims, ((), ())),
        preferred_element_type=jnp.float32,
    )


def wait_bytes(ref, sem):
    pltpu.make_async_copy(ref, ref, sem).wait()


def pair_up(row, pairs):
    shape = (pairs, row.shape[1])
    spread = jnp.broadcast_to(row, shape)
    low = jnp.sum(jnp.where(iota(shape, 1) == 2 * iota(shape, 0), spread, 0.0), axis=1, keepdims=True)
    high = jnp.sum(jnp.where(iota(shape, 1) == 2 * iota(shape, 0) + 1, spread, 0.0), axis=1, keepdims=True)
    wide = (pairs, LANES)
    return jnp.where(iota(wide, 1) < LANES // 2, jnp.broadcast_to(low, wide), jnp.broadcast_to(high, wide))


def kernel(
    n_row,
    n_col,
    residual,
    blocks,
    block_row_at,
    block_col_at,
    bins_at,
    counts_at,
    bin_scale_at,
    coarse,
    block_row,
    block_col,
    bins,
    counts,
    bin_scale,
    padded,
    res,
    blk,
    wide,
    packed,
    table,
    ask,
    asked,
    place,
    place_s,
    answer,
    got,
    terms,
    summands,
    cols,
    got_cols,
    weights,
    folded,
    load_sem,
    place_sem,
    ask_sem,
    ask_in,
    answer_sem,
    answer_in,
    term_sem,
    term_in,
    cols_sem,
    cols_in,
):
    row, col = lax.axis_index("row"), lax.axis_index("col")
    fine_dev, width = res.shape
    slots = blk.shape[0]
    cap = slots // n_row
    dofs = width // CASES
    half = dofs // 2
    groups = 2 * CASES
    tiles = blk.shape[1] // LANES

    n_z = min(RUN, n_col)
    n_y = n_col // n_z

    def col_peer(group, i):
        far = n_y - 1 - group
        step = lax.div(far + 1, 2) * (2 * lax.rem(far, 2) - 1)
        y = lax.rem(lax.div(col, n_z) + n_y // 2 + step + n_y, n_y)
        return y * n_z + lax.rem(lax.rem(col, n_z) + i + 1, n_z)

    halves = n_row // 2

    def row_peer(t):
        near = lax.div(t, halves)
        half_of = lax.rem(lax.div(row, halves) + 1 - near, 2)
        return half_of * halves + lax.rem(lax.rem(row, halves) + lax.rem(t, halves) + near, halves)

    barrier = pltpu.get_barrier_semaphore()

    def greet_col(group, i):
        pl.semaphore_signal(barrier, inc=1, device_id={"col": col_peer(group, i)}, device_id_type=MESH)

    @pl.loop(0, n_y - 1)
    def _(g):
        for i in range(n_z):
            greet_col(n_y - 1 - g, i)

    @pl.loop(0, n_row - 1)
    def _(t):
        pl.semaphore_signal(barrier, inc=1, device_id={"row": row_peer(t)}, device_id_type=MESH)

    for i in range(n_z - 1):
        greet_col(0, i)

    small = [
        pltpu.make_async_copy(a, b, load_sem.at[2 + i])
        for i, (a, b) in enumerate(
            (
                (block_row_at, block_row),
                (block_col_at, block_col),
                (bins_at, bins),
                (counts_at, counts),
                (bin_scale_at, bin_scale),
            )
        )
    ]
    for load in small:
        load.start()
    load_res = pltpu.make_async_copy(residual, res, load_sem.at[0])
    load_res.start()
    load_blk = pltpu.make_async_copy(blocks, blk, load_sem.at[1])
    load_blk.start()
    for load in small:
        load.wait()

    rows = block_row[...]
    owner = lax.div(rows, fine_dev)
    local = lax.rem(rows, fine_dev)
    square = (slots, slots)
    down, across = iota(square, 0), iota(square, 1)
    owner_down = jnp.sum(
        jnp.where(down == across, jnp.broadcast_to(owner, square), 0), axis=1, keepdims=True
    )
    rank = jnp.sum(jnp.where((owner_down == owner) & (down < across), 1, 0), axis=0, keepdims=True)
    owned = owner == iota((n_col, slots), 0)
    lane = iota((n_col, LANES), 1)
    padded[...] = jnp.zeros_like(padded)
    padded[:, 0:fine_dev] = bins[...]
    message = jnp.broadcast_to(padded[...], (n_col, LANES))
    for k in range(REQ):
        wanted = jnp.sum(jnp.where(owned & (rank == k), local, 0), axis=1, keepdims=True)
        message = jnp.where(lane == fine_dev + k, wanted, message)
    for c in range(n_col):
        ask[c] = message[c : c + 1, :]

    place[:, 0:slots] = owner * REQ + rank
    store_place = pltpu.make_async_copy(place, place_s, place_sem)
    store_place.start()

    paired = pair_up(block_col[...].astype(jnp.float32), slots // 2).astype(jnp.int32)
    for d in range(n_row):
        cols[d] = paired[d * cap // 2 : (d + 1) * cap // 2, :]

    lane = iota((1, 4 * LANES), 1)
    within = lax.rem(lane, LANES)
    group = lax.div(lane, LANES)
    source = jnp.where(within < half, lax.div(group, 2) * dofs + 2 * within + lax.rem(group, 2), -1)
    spread = (iota((2 * dofs, 4 * LANES), 0) == source).astype(jnp.bfloat16)
    load_res.wait()
    for q in range(CASES // 2):
        two = dot(res[:, 2 * dofs * q : 2 * dofs * (q + 1)], spread)
        for g in range(4):
            at = (g % 2) * CASES + 2 * q + g // 2
            wide[pl.ds(at, fine_dev, stride=groups), :] = two[:, g * LANES : (g + 1) * LANES]
    table[...] = wide[0 : fine_dev * groups, :].reshape(fine_dev, groups, LANES)

    pl.semaphore_wait(barrier, n_col + n_row - 2)

    def to_col(src, dst, send, recv, peer):
        return pltpu.make_async_remote_copy(
            src_ref=src, dst_ref=dst, send_sem=send, recv_sem=recv, device_id={"col": peer}, device_id_type=MESH
        )

    def to_row(src, dst, send, recv, peer):
        return pltpu.make_async_remote_copy(
            src_ref=src, dst_ref=dst, send_sem=send, recv_sem=recv, device_id={"row": peer}, device_id_type=MESH
        )

    def request(group, i):
        peer = col_peer(group, i)
        to_col(ask.at[peer], asked.at[col], ask_sem, ask_in.at[col], peer).start()

    @pl.loop(0, n_y - 1)
    def _(g):
        for i in range(n_z):
            request(n_y - 1 - g, i)

    for i in range(n_z - 1):
        request(0, i)

    asked[col] = ask[col]

    @pl.loop(0, n_row - 1)
    def _(t):
        peer = row_peer(t)
        to_row(cols.at[peer], got_cols.at[row], cols_sem, cols_in.at[row], peer).start()

    got_cols[row] = cols[row]

    thirds = LANES - half
    low_lanes = iota((groups, LANES), 1) < half

    def rows_for(peer):
        picked = []
        for k in range(REQ):
            picked.append(table[asked[peer, 0, fine_dev + k]])
        return [
            jnp.where(low_lanes, picked[v], pltpu.roll(picked[3], half - thirds * v, 1)).astype(jnp.bfloat16)
            for v in range(3)
        ]

    def take(group, count):
        peers = [col_peer(group, i) for i in range(n_z)]
        for peer in peers[:count]:
            wait_bytes(asked.at[peer], ask_in.at[peer])

    def reply(group, count):
        peers = [col_peer(group, i) for i in range(n_z)]
        filled = [rows_for(peer) for peer in peers]
        for peer, rows_of in zip(peers[:count], filled):
            for v, tile in enumerate(rows_of):
                answer[peer, v] = tile
            to_col(
                answer.at[peer], got.at[pl.ds(col * REQ, 3)], answer_sem, answer_in.at[col], peer
            ).start()
        if count < n_z:
            for v, tile in enumerate(filled[-1]):
                got[col * REQ + v] = tile

    take(0, n_z - 1)
    reply(0, n_z - 1)

    @pl.loop(1, n_y)
    def _(g):
        take(g, n_z)
        reply(g, n_z)

    load_blk.wait()

    @pl.loop(0, tiles, unroll=4)
    def _(t):
        at = pl.multiple_of(t * LANES, LANES)
        wide[pl.ds(t, slots, stride=tiles), :] = blk[:, pl.ds(at, LANES)].astype(jnp.float32)

    @pl.loop(0, slots)
    def _(s):
        at = pl.multiple_of(s * tiles, 8)
        packed[s, 0:half, :] = wide[pl.ds(at, half), :].astype(jnp.bfloat16)
        packed[s, half:, :] = jnp.zeros((LANES - half, LANES), jnp.bfloat16)

    all_bins = asked[...].reshape(n_col, LANES).astype(jnp.float32)
    here = (local == iota((LANES, slots), 0)).astype(jnp.float32)
    bin_of = jnp.sum(jnp.where(owned, dot(all_bins, here), 0.0), axis=0, keepdims=True).astype(jnp.int32)
    n_bins = bin_scale.shape[1]
    square = (n_bins, n_bins)
    scales = jnp.sum(
        jnp.where(iota(square, 0) == iota(square, 1), jnp.broadcast_to(bin_scale[...], square), 0.0),
        axis=1,
        keepdims=True,
    )
    scale_of = jnp.sum(jnp.where(bin_of == iota((n_bins, slots), 0), scales, 0.0), axis=0, keepdims=True)
    of_bucket = (lax.div(iota((n_row, slots), 1), cap) == iota((n_row, slots), 0)).astype(jnp.float32)
    live = lax.rem(iota((1, slots), 1), cap).astype(jnp.float32) < dot(counts[...].astype(jnp.float32), of_bucket)
    weights[...] = pair_up(jnp.where(live, scale_of, 0.0), slots // 2)

    store_place.wait()
    lane_at = iota((groups, LANES), 1)

    def gather_thirds(group, count):
        peers = [col_peer(group, i) for i in range(n_z)]
        for peer in peers[:count]:
            wait_bytes(got.at[pl.ds(peer * REQ, 3)], answer_in.at[peer])
        joined = []
        for peer in peers:
            a, b, d = (
                pltpu.roll(got[peer * REQ + v].astype(jnp.float32), thirds * (v + 1), 1) for v in range(3)
            )
            joined.append(jnp.where(lane_at < thirds, a, jnp.where(lane_at < 2 * thirds, b, d)))
        for peer, tile in zip(peers, joined):
            got[peer * REQ + 3] = tile.astype(jnp.bfloat16)

    gather_thirds(0, n_z - 1)

    @pl.loop(1, n_y)
    def _(g):
        gather_thirds(g, n_z)

    low = iota((CASES, LANES), 1) < LANES // 2

    def term(slot):
        panel = got[place_s[0, slot]]
        both = jnp.dot(panel, packed[slot], preferred_element_type=jnp.float32)
        return both[:CASES], both[CASES:]

    def bucket(d):
        pairs = []
        for pair in range(cap // 2):
            a0, a1 = term(d * cap + 2 * pair)
            b0, b1 = term(d * cap + 2 * pair + 1)
            both = jnp.where(low, a0, b1) + pltpu.roll(jnp.where(low, b0, a1), LANES // 2, 1)
            pairs.append(both * weights[pl.ds(d * (cap // 2) + pair, 1), :])
        return pairs

    def store(dest, at, pairs):
        for pair, value in enumerate(pairs):
            dest[at, pair * CASES : (pair + 1) * CASES, :] = value

    def send(peers, summed):
        for peer, pairs in zip(peers, summed):
            store(terms, peer, pairs)
            to_row(terms.at[peer], summands.at[row], term_sem, term_in.at[row], peer).start()

    together = min(4, n_row)

    @pl.loop(0, n_row // together - 1)
    def _(g):
        peers = [row_peer(g * together + i) for i in range(together)]
        send(peers, [bucket(d) for d in peers])

    peers = [row_peer(n_row - together + i) for i in range(together - 1)]
    summed = [bucket(d) for d in peers + [row]]
    send(peers, summed[:-1])
    store(summands, row, summed[-1])

    def add(r, sums):
        for pair in range(cap // 2):
            value = summands[r, pair * CASES : (pair + 1) * CASES, :]
            to = got_cols[r, pair : pair + 1, :]
            sums = tuple(s + jnp.where(to == a, value, 0.0) for a, s in enumerate(sums))
        return sums

    def arrive(t, sums):
        peer = row_peer(n_row - 2 - t)
        wait_bytes(got_cols.at[peer], cols_in.at[peer])
        wait_bytes(summands.at[peer], term_in.at[peer])
        return add(peer, sums)

    sums = add(row, (jnp.zeros((CASES, LANES), jnp.float32),) * AG_DEV)
    sums = lax.fori_loop(0, n_row - 1, arrive, sums)
    for a, s in enumerate(sums):
        s = s + pltpu.roll(s, LANES // 2, 1)
        folded[a * CASES : (a + 1) * CASES, :] = jnp.where(low, s, pltpu.roll(s, CASES - 1, 0))
    for j in range(CASES // 2):
        coarse[:, j * LANES : (j + 1) * LANES] = folded[pl.ds(2 * j, AG_DEV, stride=CASES), :]

    wait_bytes(ask.at[pl.ds(0, n_col - 1)], ask_sem)
    wait_bytes(cols.at[pl.ds(0, n_row - 1)], cols_sem)
    wait_bytes(answer.at[pl.ds(0, n_col - 1)], answer_sem)
    wait_bytes(terms.at[pl.ds(0, n_row - 1)], term_sem)


def shards(n_row, n_col, residual, bins, bin_scale, blocks, block_row, block_col, counts):
    slots, entries = blocks.shape
    fine_dev, width = residual.shape
    cap = slots // n_row
    dofs = width // CASES
    aggregate = entries // dofs
    tiles = entries // LANES
    f32, bf16, i32 = jnp.float32, jnp.bfloat16, jnp.int32
    vmem = pl.BlockSpec(memory_space=pltpu.VMEM)
    hbm = pl.BlockSpec(memory_space=pltpu.HBM)
    dma = pltpu.SemaphoreType.DMA
    out = pl.pallas_call(
        functools.partial(kernel, n_row, n_col),
        out_shape=jax.ShapeDtypeStruct((AG_DEV, CASES * aggregate), f32),
        in_specs=[hbm] * 7,
        out_specs=vmem,
        scratch_shapes=[
            pltpu.VMEM((1, slots), i32),
            pltpu.VMEM((1, slots), i32),
            pltpu.VMEM((1, fine_dev), i32),
            pltpu.VMEM((1, n_row), i32),
            pltpu.VMEM((1, bin_scale.shape[0]), f32),
            pltpu.VMEM((1, LANES), i32),
            pltpu.VMEM((fine_dev, width), bf16),
            pltpu.VMEM((slots, entries), bf16),
            pltpu.VMEM((slots * tiles, LANES), f32),
            pltpu.VMEM((slots, LANES, LANES), bf16),
            pltpu.VMEM((fine_dev, 2 * CASES, LANES), f32),
            pltpu.VMEM((n_col, 1, LANES), i32),
            pltpu.VMEM((n_col, 1, LANES), i32),
            pltpu.VMEM((1, LANES), i32),
            pltpu.SMEM((1, LANES), i32),
            pltpu.VMEM((n_col, 3, 2 * CASES, LANES), bf16),
            pltpu.VMEM((n_col * REQ, 2 * CASES, LANES), bf16),
            pltpu.VMEM((n_row, cap // 2 * CASES, LANES), f32),
            pltpu.VMEM((n_row, cap // 2 * CASES, LANES), f32),
            pltpu.VMEM((n_row, cap // 2, LANES), i32),
            pltpu.VMEM((n_row, cap // 2, LANES), i32),
            pltpu.VMEM((slots // 2, LANES), f32),
            pltpu.VMEM((AG_DEV * CASES, LANES), f32),
            dma((7,)),
        ]
        + [dma, dma, dma((n_col,)), dma, dma((n_col,))]
        + [dma, dma((n_row,)), dma, dma((n_row,))],
        compiler_params=pltpu.CompilerParams(
            collective_id=0, has_side_effects=True, vmem_limit_bytes=32 * 1024 * 1024
        ),
    )(
        *(
            pltpu.with_memory_space_constraint(a, pltpu.HBM)
            for a in (
                residual,
                blocks,
                block_row.reshape(1, -1),
                block_col.reshape(1, -1),
                bins.reshape(1, -1),
                counts.reshape(1, -1),
                bin_scale.reshape(1, -1),
            )
        )
    )
    return out[None]


def solution(mesh):
    both = P(("row", "col"))
    rows = P(("row", "col"), None)
    return jax.shard_map(
        functools.partial(shards, mesh.shape["row"], mesh.shape["col"]),
        mesh=mesh,
        in_specs=(rows, both, P(), rows, both, both, both),
        out_specs=P("col", "row", None),
        check_vma=False,
    )
```

```python
import functools

import jax
import jax.numpy as jnp
from jax import lax
from jax.experimental import pallas as pl
from jax.experimental.pallas import tpu as pltpu
from jax.sharding import PartitionSpec as P

CASES = 8
AG_DEV = 8
REQ = 4
LANES = 128
RUN = 4
MESH = pl.DeviceIdType.MESH


def iota(shape, dim):
    return lax.broadcasted_iota(jnp.int32, shape, dim)


def dot(a, b, dims=((1,), (0,))):
    return lax.dot_general(
        a.astype(jnp.bfloat16),
        b.astype(jnp.bfloat16),
        (dims, ((), ())),
        preferred_element_type=jnp.float32,
    )


def wait_bytes(ref, sem):
    pltpu.make_async_copy(ref, ref, sem).wait()


def pair_up(row, pairs):
    shape = (pairs, row.shape[1])
    spread = jnp.broadcast_to(row, shape)
    low = jnp.sum(jnp.where(iota(shape, 1) == 2 * iota(shape, 0), spread, 0.0), axis=1, keepdims=True)
    high = jnp.sum(jnp.where(iota(shape, 1) == 2 * iota(shape, 0) + 1, spread, 0.0), axis=1, keepdims=True)
    wide = (pairs, LANES)
    return jnp.where(iota(wide, 1) < LANES // 2, jnp.broadcast_to(low, wide), jnp.broadcast_to(high, wide))


def kernel(
    n_row,
    n_col,
    residual,
    blocks,
    block_row_at,
    block_col_at,
    bins_at,
    counts_at,
    bin_scale_at,
    coarse,
    block_row,
    block_col,
    bins,
    counts,
    bin_scale,
    padded,
    res,
    blk,
    wide,
    packed,
    table,
    ask,
    asked,
    place,
    place_s,
    answer,
    got,
    terms,
    summands,
    cols,
    got_cols,
    weights,
    folded,
    load_sem,
    place_sem,
    ask_sem,
    ask_in,
    answer_sem,
    answer_in,
    term_sem,
    term_in,
    cols_sem,
    cols_in,
):
    row, col = lax.axis_index("row"), lax.axis_index("col")
    fine_dev, width = res.shape
    slots = blk.shape[0]
    cap = slots // n_row
    dofs = width // CASES
    half = dofs // 2
    groups = 2 * CASES
    tiles = blk.shape[1] // LANES

    n_z = min(RUN, n_col)
    n_y = n_col // n_z

    def col_peer(group, i):
        far = n_y - 1 - group
        step = lax.div(far + 1, 2) * (2 * lax.rem(far, 2) - 1)
        y = lax.rem(lax.div(col, n_z) + n_y // 2 + step + n_y, n_y)
        return y * n_z + lax.rem(lax.rem(col, n_z) + i + 1, n_z)

    halves = n_row // 2

    def row_peer(t):
        near = lax.div(t, halves)
        half_of = lax.rem(lax.div(row, halves) + 1 - near, 2)
        return half_of * halves + lax.rem(lax.rem(row, halves) + lax.rem(t, halves) + near, halves)

    barrier = pltpu.get_barrier_semaphore()

    def greet_col(group, i):
        pl.semaphore_signal(barrier, inc=1, device_id={"col": col_peer(group, i)}, device_id_type=MESH)

    def greet_row(t):
        pl.semaphore_signal(barrier, inc=1, device_id={"row": row_peer(t)}, device_id_type=MESH)

    if n_y > 1:
        for i in range(n_z):
            greet_col(n_y - 1, i)

    @pl.loop(0, halves)
    def _(t):
        greet_row(t)

    @pl.loop(1, n_y - 1)
    def _(g):
        for i in range(n_z):
            greet_col(n_y - 1 - g, i)

    @pl.loop(halves, n_row - 1)
    def _(t):
        greet_row(t)

    for i in range(n_z - 1):
        greet_col(0, i)

    small = [
        pltpu.make_async_copy(a, b, load_sem.at[2 + i])
        for i, (a, b) in enumerate(
            (
                (block_row_at, block_row),
                (block_col_at, block_col),
                (bins_at, bins),
                (counts_at, counts),
                (bin_scale_at, bin_scale),
            )
        )
    ]
    for load in small:
        load.start()
    load_res = pltpu.make_async_copy(residual, res, load_sem.at[0])
    load_res.start()
    load_blk = pltpu.make_async_copy(blocks, blk, load_sem.at[1])
    load_blk.start()
    for load in small:
        load.wait()

    rows = block_row[...]
    owner = lax.div(rows, fine_dev)
    local = lax.rem(rows, fine_dev)
    square = (slots, slots)
    down, across = iota(square, 0), iota(square, 1)
    owner_down = jnp.sum(
        jnp.where(down == across, jnp.broadcast_to(owner, square), 0), axis=1, keepdims=True
    )
    rank = jnp.sum(jnp.where((owner_down == owner) & (down < across), 1, 0), axis=0, keepdims=True)
    owned = owner == iota((n_col, slots), 0)
    lane = iota((n_col, LANES), 1)
    padded[...] = jnp.zeros_like(padded)
    padded[:, 0:fine_dev] = bins[...]
    message = jnp.broadcast_to(padded[...], (n_col, LANES))
    for k in range(REQ):
        wanted = jnp.sum(jnp.where(owned & (rank == k), local, 0), axis=1, keepdims=True)
        message = jnp.where(lane == fine_dev + k, wanted, message)
    for c in range(n_col):
        ask[c] = message[c : c + 1, :]

    place[:, 0:slots] = owner * REQ + rank
    store_place = pltpu.make_async_copy(place, place_s, place_sem)
    store_place.start()

    paired = pair_up(block_col[...].astype(jnp.float32), slots // 2).astype(jnp.int32)
    for d in range(n_row):
        cols[d] = paired[d * cap // 2 : (d + 1) * cap // 2, :]

    lane = iota((1, 4 * LANES), 1)
    within = lax.rem(lane, LANES)
    group = lax.div(lane, LANES)
    source = jnp.where(within < half, lax.div(group, 2) * dofs + 2 * within + lax.rem(group, 2), -1)
    spread = (iota((2 * dofs, 4 * LANES), 0) == source).astype(jnp.bfloat16)
    load_res.wait()
    for q in range(CASES // 2):
        two = dot(res[:, 2 * dofs * q : 2 * dofs * (q + 1)], spread)
        for g in range(4):
            at = (g % 2) * CASES + 2 * q + g // 2
            wide[pl.ds(at, fine_dev, stride=groups), :] = two[:, g * LANES : (g + 1) * LANES]
    table[...] = wide[0 : fine_dev * groups, :].reshape(fine_dev, groups, LANES)

    pl.semaphore_wait(barrier, n_col + n_row - 2)

    def to_col(src, dst, send, recv, peer):
        return pltpu.make_async_remote_copy(
            src_ref=src, dst_ref=dst, send_sem=send, recv_sem=recv, device_id={"col": peer}, device_id_type=MESH
        )

    def to_row(src, dst, send, recv, peer):
        return pltpu.make_async_remote_copy(
            src_ref=src, dst_ref=dst, send_sem=send, recv_sem=recv, device_id={"row": peer}, device_id_type=MESH
        )

    def request(group, i):
        peer = col_peer(group, i)
        to_col(ask.at[peer], asked.at[col], ask_sem, ask_in.at[col], peer).start()

    @pl.loop(0, n_y - 1)
    def _(g):
        for i in range(n_z):
            request(n_y - 1 - g, i)

    for i in range(n_z - 1):
        request(0, i)

    asked[col] = ask[col]

    @pl.loop(0, n_row - 1)
    def _(t):
        peer = row_peer(t)
        to_row(cols.at[peer], got_cols.at[row], cols_sem, cols_in.at[row], peer).start()

    got_cols[row] = cols[row]

    thirds = LANES - half
    low_lanes = iota((groups, LANES), 1) < half

    def rows_for(peer):
        picked = []
        for k in range(REQ):
            picked.append(table[asked[peer, 0, fine_dev + k]])
        return [
            jnp.where(low_lanes, picked[v], pltpu.roll(picked[3], half - thirds * v, 1)).astype(jnp.bfloat16)
            for v in range(3)
        ]

    def take(group, count):
        peers = [col_peer(group, i) for i in range(n_z)]
        for peer in peers[:count]:
            wait_bytes(asked.at[peer], ask_in.at[peer])

    def reply(group, count):
        peers = [col_peer(group, i) for i in range(n_z)]
        filled = [rows_for(peer) for peer in peers]
        for peer, rows_of in zip(peers[:count], filled):
            for v, tile in enumerate(rows_of):
                answer[peer, v] = tile
            to_col(
                answer.at[peer], got.at[pl.ds(col * REQ, 3)], answer_sem, answer_in.at[col], peer
            ).start()
        if count < n_z:
            for v, tile in enumerate(filled[-1]):
                got[col * REQ + v] = tile

    take(0, n_z - 1)
    reply(0, n_z - 1)

    @pl.loop(1, n_y)
    def _(g):
        take(g, n_z)
        reply(g, n_z)

    load_blk.wait()

    @pl.loop(0, tiles, unroll=4)
    def _(t):
        at = pl.multiple_of(t * LANES, LANES)
        wide[pl.ds(t, slots, stride=tiles + 1), :] = blk[:, pl.ds(at, LANES)].astype(jnp.float32)

    @pl.loop(0, slots)
    def _(s):
        packed[s, 0:half, :] = wide[pl.ds(s * (tiles + 1), half), :].astype(jnp.bfloat16)
        packed[s, half:, :] = jnp.zeros((LANES - half, LANES), jnp.bfloat16)

    all_bins = asked[...].reshape(n_col, LANES).astype(jnp.float32)
    here = (local == iota((LANES, slots), 0)).astype(jnp.float32)
    bin_of = jnp.sum(jnp.where(owned, dot(all_bins, here), 0.0), axis=0, keepdims=True).astype(jnp.int32)
    n_bins = bin_scale.shape[1]
    square = (n_bins, n_bins)
    scales = jnp.sum(
        jnp.where(iota(square, 0) == iota(square, 1), jnp.broadcast_to(bin_scale[...], square), 0.0),
        axis=1,
        keepdims=True,
    )
    scale_of = jnp.sum(jnp.where(bin_of == iota((n_bins, slots), 0), scales, 0.0), axis=0, keepdims=True)
    of_bucket = (lax.div(iota((n_row, slots), 1), cap) == iota((n_row, slots), 0)).astype(jnp.float32)
    live = lax.rem(iota((1, slots), 1), cap).astype(jnp.float32) < dot(counts[...].astype(jnp.float32), of_bucket)
    weights[...] = pair_up(jnp.where(live, scale_of, 0.0), slots // 2)

    store_place.wait()
    lane_at = iota((groups, LANES), 1)

    def gather_thirds(group, count):
        peers = [col_peer(group, i) for i in range(n_z)]
        for peer in peers[:count]:
            wait_bytes(got.at[pl.ds(peer * REQ, 3)], answer_in.at[peer])
        joined = []
        for peer in peers:
            a, b, d = (
                pltpu.roll(got[peer * REQ + v].astype(jnp.float32), thirds * (v + 1), 1) for v in range(3)
            )
            joined.append(jnp.where(lane_at < thirds, a, jnp.where(lane_at < 2 * thirds, b, d)))
        for peer, tile in zip(peers, joined):
            got[peer * REQ + 3] = tile.astype(jnp.bfloat16)

    gather_thirds(0, n_z - 1)

    @pl.loop(1, n_y)
    def _(g):
        gather_thirds(g, n_z)

    low = iota((CASES, LANES), 1) < LANES // 2

    def term(slot):
        panel = got[place_s[0, slot]]
        both = jnp.dot(panel, packed[slot], preferred_element_type=jnp.float32)
        return both[:CASES], both[CASES:]

    def bucket(d):
        pairs = []
        for pair in range(cap // 2):
            a0, a1 = term(d * cap + 2 * pair)
            b0, b1 = term(d * cap + 2 * pair + 1)
            both = jnp.where(low, a0, b1) + pltpu.roll(jnp.where(low, b0, a1), LANES // 2, 1)
            pairs.append(both * weights[pl.ds(d * (cap // 2) + pair, 1), :])
        return pairs

    def store(dest, at, pairs):
        for pair, value in enumerate(pairs):
            dest[at, pair * CASES : (pair + 1) * CASES, :] = value

    def send(peers, summed):
        for peer, pairs in zip(peers, summed):
            store(terms, peer, pairs)
            to_row(terms.at[peer], summands.at[row], term_sem, term_in.at[row], peer).start()

    together = min(4, n_row)

    @pl.loop(0, n_row // together - 1)
    def _(g):
        peers = [row_peer(g * together + i) for i in range(together)]
        send(peers, [bucket(d) for d in peers])

    peers = [row_peer(n_row - together + i) for i in range(together - 1)]
    summed = [bucket(d) for d in peers + [row]]
    send(peers, summed[:-1])
    store(summands, row, summed[-1])

    def add(r, sums):
        for pair in range(cap // 2):
            value = summands[r, pair * CASES : (pair + 1) * CASES, :]
            to = got_cols[r, pair : pair + 1, :]
            sums = tuple(s + jnp.where(to == a, value, 0.0) for a, s in enumerate(sums))
        return sums

    @pl.loop(0, n_row - 1)
    def _(t):
        peer = row_peer(t)
        wait_bytes(got_cols.at[peer], cols_in.at[peer])

    def arrive(peers, sums):
        for peer in peers:
            wait_bytes(summands.at[peer], term_in.at[peer])
        for peer in peers:
            sums = add(peer, sums)
        return sums

    def group_of(g):
        return [row_peer(n_row - 1 - g * together - i) for i in range(together)]

    sums = add(row, (jnp.zeros((CASES, LANES), jnp.float32),) * AG_DEV)
    sums = arrive(group_of(0)[1:], sums)
    sums = lax.fori_loop(1, n_row // together, lambda g, sums: arrive(group_of(g), sums), sums)
    for a, s in enumerate(sums):
        s = s + pltpu.roll(s, LANES // 2, 1)
        folded[a * CASES : (a + 1) * CASES, :] = jnp.where(low, s, pltpu.roll(s, CASES - 1, 0))
    for j in range(CASES // 2):
        coarse[:, j * LANES : (j + 1) * LANES] = folded[pl.ds(2 * j, AG_DEV, stride=CASES), :]

    wait_bytes(ask.at[pl.ds(0, n_col - 1)], ask_sem)
    wait_bytes(cols.at[pl.ds(0, n_row - 1)], cols_sem)
    wait_bytes(answer.at[pl.ds(0, n_col - 1)], answer_sem)
    wait_bytes(terms.at[pl.ds(0, n_row - 1)], term_sem)


def shards(n_row, n_col, residual, bins, bin_scale, blocks, block_row, block_col, counts):
    slots, entries = blocks.shape
    fine_dev, width = residual.shape
    cap = slots // n_row
    dofs = width // CASES
    aggregate = entries // dofs
    tiles = entries // LANES
    f32, bf16, i32 = jnp.float32, jnp.bfloat16, jnp.int32
    vmem = pl.BlockSpec(memory_space=pltpu.VMEM)
    hbm = pl.BlockSpec(memory_space=pltpu.HBM)
    dma = pltpu.SemaphoreType.DMA
    out = pl.pallas_call(
        functools.partial(kernel, n_row, n_col),
        out_shape=jax.ShapeDtypeStruct((AG_DEV, CASES * aggregate), f32),
        in_specs=[hbm] * 7,
        out_specs=vmem,
        scratch_shapes=[
            pltpu.VMEM((1, slots), i32),
            pltpu.VMEM((1, slots), i32),
            pltpu.VMEM((1, fine_dev), i32),
            pltpu.VMEM((1, n_row), i32),
            pltpu.VMEM((1, bin_scale.shape[0]), f32),
            pltpu.VMEM((1, LANES), i32),
            pltpu.VMEM((fine_dev, width), bf16),
            pltpu.VMEM((slots, entries), bf16),
            pltpu.VMEM(((slots + 1) * (tiles + 1), LANES), f32),
            pltpu.VMEM((slots, LANES, LANES), bf16),
            pltpu.VMEM((fine_dev, 2 * CASES, LANES), f32),
            pltpu.VMEM((n_col, 1, LANES), i32),
            pltpu.VMEM((n_col, 1, LANES), i32),
            pltpu.VMEM((1, LANES), i32),
            pltpu.SMEM((1, LANES), i32),
            pltpu.VMEM((n_col, 3, 2 * CASES, LANES), bf16),
            pltpu.VMEM((n_col * REQ, 2 * CASES, LANES), bf16),
            pltpu.VMEM((n_row, cap // 2 * CASES, LANES), f32),
            pltpu.VMEM((n_row, cap // 2 * CASES, LANES), f32),
            pltpu.VMEM((n_row, cap // 2, LANES), i32),
            pltpu.VMEM((n_row, cap // 2, LANES), i32),
            pltpu.VMEM((slots // 2, LANES), f32),
            pltpu.VMEM(((AG_DEV + 1) * CASES, LANES), f32),
            dma((7,)),
        ]
        + [dma, dma, dma((n_col,)), dma, dma((n_col,))]
        + [dma, dma((n_row,)), dma, dma((n_row,))],
        compiler_params=pltpu.CompilerParams(
            collective_id=0, has_side_effects=True, vmem_limit_bytes=32 * 1024 * 1024
        ),
    )(
        *(
            pltpu.with_memory_space_constraint(a, pltpu.HBM)
            for a in (
                residual,
                blocks,
                block_row.reshape(1, -1),
                block_col.reshape(1, -1),
                bins.reshape(1, -1),
                counts.reshape(1, -1),
                bin_scale.reshape(1, -1),
            )
        )
    )
    return out[None]


def solution(mesh):
    both = P(("row", "col"))
    rows = P(("row", "col"), None)
    return jax.shard_map(
        functools.partial(shards, mesh.shape["row"], mesh.shape["col"]),
        mesh=mesh,
        in_specs=(rows, both, P(), rows, both, both, both),
        out_specs=P("col", "row", None),
        check_vma=False,
    )
```

```python
import functools

import jax
import jax.numpy as jnp
from jax import lax
from jax.experimental import pallas as pl
from jax.experimental.pallas import tpu as pltpu
from jax.sharding import PartitionSpec as P

CASES = 8
AG_DEV = 8
REQ = 4
LANES = 128
RUN = 4
MESH = pl.DeviceIdType.MESH


def iota(shape, dim):
    return lax.broadcasted_iota(jnp.int32, shape, dim)


def dot(a, b, dims=((1,), (0,))):
    return lax.dot_general(
        a.astype(jnp.bfloat16),
        b.astype(jnp.bfloat16),
        (dims, ((), ())),
        preferred_element_type=jnp.float32,
    )


def wait_bytes(ref, sem):
    pltpu.make_async_copy(ref, ref, sem).wait()


def pair_up(row, pairs):
    shape = (pairs, row.shape[1])
    spread = jnp.broadcast_to(row, shape)
    low = jnp.sum(jnp.where(iota(shape, 1) == 2 * iota(shape, 0), spread, 0.0), axis=1, keepdims=True)
    high = jnp.sum(jnp.where(iota(shape, 1) == 2 * iota(shape, 0) + 1, spread, 0.0), axis=1, keepdims=True)
    wide = (pairs, LANES)
    return jnp.where(iota(wide, 1) < LANES // 2, jnp.broadcast_to(low, wide), jnp.broadcast_to(high, wide))


def kernel(
    n_row,
    n_col,
    residual,
    blocks,
    block_row_at,
    block_col_at,
    bins_at,
    counts_at,
    bin_scale_at,
    coarse,
    block_row,
    block_col,
    bins,
    counts,
    bin_scale,
    padded,
    res,
    blk,
    wide,
    packed,
    table,
    ask,
    asked,
    place,
    place_s,
    answer,
    got,
    terms,
    summands,
    cols,
    got_cols,
    weights,
    folded,
    load_sem,
    place_sem,
    ask_sem,
    ask_in,
    answer_sem,
    answer_in,
    term_sem,
    term_in,
    cols_sem,
    cols_in,
):
    row, col = lax.axis_index("row"), lax.axis_index("col")
    fine_dev, width = res.shape
    slots = blk.shape[0]
    cap = slots // n_row
    dofs = width // CASES
    half = dofs // 2
    groups = 2 * CASES
    tiles = blk.shape[1] // LANES

    n_z = min(RUN, n_col)
    n_y = n_col // n_z

    def col_peer(group, i):
        far = n_y - 1 - group
        step = lax.div(far + 1, 2) * (2 * lax.rem(far, 2) - 1)
        y = lax.rem(lax.div(col, n_z) + n_y // 2 + step + n_y, n_y)
        return y * n_z + lax.rem(lax.rem(col, n_z) + i + 1, n_z)

    halves = n_row // 2

    def row_peer(t):
        near = lax.div(t, halves)
        half_of = lax.rem(lax.div(row, halves) + 1 - near, 2)
        ahead = near + (1 - near) * max(halves // 2 - 1, 0)
        return half_of * halves + lax.rem(lax.rem(row, halves) + lax.rem(t, halves) + ahead, halves)

    barrier = pltpu.get_barrier_semaphore()

    def greet_col(group, i):
        pl.semaphore_signal(barrier, inc=1, device_id={"col": col_peer(group, i)}, device_id_type=MESH)

    def greet_row(t):
        pl.semaphore_signal(barrier, inc=1, device_id={"row": row_peer(t)}, device_id_type=MESH)

    if n_y > 1:
        for i in range(n_z):
            greet_col(n_y - 1, i)

    @pl.loop(0, halves)
    def _(t):
        greet_row(t)

    @pl.loop(1, n_y - 1)
    def _(g):
        for i in range(n_z):
            greet_col(n_y - 1 - g, i)

    @pl.loop(halves, n_row - 1)
    def _(t):
        greet_row(t)

    for i in range(n_z - 1):
        greet_col(0, i)

    small = [
        pltpu.make_async_copy(a, b, load_sem.at[2 + i])
        for i, (a, b) in enumerate(
            (
                (block_row_at, block_row),
                (block_col_at, block_col),
                (bins_at, bins),
                (counts_at, counts),
                (bin_scale_at, bin_scale),
            )
        )
    ]
    for load in small:
        load.start()
    load_res = pltpu.make_async_copy(residual, res, load_sem.at[0])
    load_res.start()
    load_blk = pltpu.make_async_copy(blocks, blk, load_sem.at[1])
    load_blk.start()
    for load in small:
        load.wait()

    rows = block_row[...]
    owner = lax.div(rows, fine_dev)
    local = lax.rem(rows, fine_dev)
    square = (slots, slots)
    down, across = iota(square, 0), iota(square, 1)
    owner_down = jnp.sum(
        jnp.where(down == across, jnp.broadcast_to(owner, square), 0), axis=1, keepdims=True
    )
    rank = jnp.sum(jnp.where((owner_down == owner) & (down < across), 1, 0), axis=0, keepdims=True)
    owned = owner == iota((n_col, slots), 0)
    lane = iota((n_col, LANES), 1)
    padded[...] = jnp.zeros_like(padded)
    padded[:, 0:fine_dev] = bins[...]
    message = jnp.broadcast_to(padded[...], (n_col, LANES))
    for k in range(REQ):
        wanted = jnp.sum(jnp.where(owned & (rank == k), local, 0), axis=1, keepdims=True)
        message = jnp.where(lane == fine_dev + k, wanted, message)
    for c in range(n_col):
        ask[c] = message[c : c + 1, :]

    place[:, 0:slots] = owner * REQ + rank
    store_place = pltpu.make_async_copy(place, place_s, place_sem)
    store_place.start()

    paired = pair_up(block_col[...].astype(jnp.float32), slots // 2).astype(jnp.int32)
    for d in range(n_row):
        cols[d] = paired[d * cap // 2 : (d + 1) * cap // 2, :]

    lane = iota((1, 4 * LANES), 1)
    within = lax.rem(lane, LANES)
    group = lax.div(lane, LANES)
    source = jnp.where(within < half, lax.div(group, 2) * dofs + 2 * within + lax.rem(group, 2), -1)
    spread = (iota((2 * dofs, 4 * LANES), 0) == source).astype(jnp.bfloat16)
    load_res.wait()
    for q in range(CASES // 2):
        two = dot(res[:, 2 * dofs * q : 2 * dofs * (q + 1)], spread)
        for g in range(4):
            at = (g % 2) * CASES + 2 * q + g // 2
            wide[pl.ds(at, fine_dev, stride=groups), :] = two[:, g * LANES : (g + 1) * LANES]
    table[...] = wide[0 : fine_dev * groups, :].reshape(fine_dev, groups, LANES)

    pl.semaphore_wait(barrier, n_col + n_row - 2)

    def to_col(src, dst, send, recv, peer):
        return pltpu.make_async_remote_copy(
            src_ref=src, dst_ref=dst, send_sem=send, recv_sem=recv, device_id={"col": peer}, device_id_type=MESH
        )

    def to_row(src, dst, send, recv, peer):
        return pltpu.make_async_remote_copy(
            src_ref=src, dst_ref=dst, send_sem=send, recv_sem=recv, device_id={"row": peer}, device_id_type=MESH
        )

    def request(group, i):
        peer = col_peer(group, i)
        to_col(ask.at[peer], asked.at[col], ask_sem, ask_in.at[col], peer).start()

    @pl.loop(0, n_y - 1)
    def _(g):
        for i in range(n_z):
            request(n_y - 1 - g, i)

    for i in range(n_z - 1):
        request(0, i)

    asked[col] = ask[col]

    @pl.loop(0, n_row - 1)
    def _(t):
        peer = row_peer(t)
        to_row(cols.at[peer], got_cols.at[row], cols_sem, cols_in.at[row], peer).start()

    got_cols[row] = cols[row]

    thirds = LANES - half
    low_lanes = iota((groups, LANES), 1) < half

    def rows_for(peer):
        picked = []
        for k in range(REQ):
            picked.append(table[asked[peer, 0, fine_dev + k]])
        return [
            jnp.where(low_lanes, picked[v], pltpu.roll(picked[3], half - thirds * v, 1)).astype(jnp.bfloat16)
            for v in range(3)
        ]

    def take(group, count):
        peers = [col_peer(group, i) for i in range(n_z)]
        for peer in peers[:count]:
            wait_bytes(asked.at[peer], ask_in.at[peer])

    def reply(group, count):
        peers = [col_peer(group, i) for i in range(n_z)]
        filled = [rows_for(peer) for peer in peers]
        for peer, rows_of in zip(peers[:count], filled):
            for v, tile in enumerate(rows_of):
                answer[peer, v] = tile
            to_col(
                answer.at[peer], got.at[pl.ds(col * REQ, 3)], answer_sem, answer_in.at[col], peer
            ).start()
        if count < n_z:
            for v, tile in enumerate(filled[-1]):
                got[col * REQ + v] = tile

    take(0, n_z - 1)
    reply(0, n_z - 1)

    @pl.loop(1, n_y)
    def _(g):
        take(g, n_z)
        reply(g, n_z)

    load_blk.wait()

    @pl.loop(0, tiles, unroll=4)
    def _(t):
        at = pl.multiple_of(t * LANES, LANES)
        wide[pl.ds(t, slots, stride=tiles + 1), :] = blk[:, pl.ds(at, LANES)].astype(jnp.float32)

    @pl.loop(0, slots)
    def _(s):
        packed[s, 0:half, :] = wide[pl.ds(s * (tiles + 1), half), :].astype(jnp.bfloat16)
        packed[s, half:, :] = jnp.zeros((LANES - half, LANES), jnp.bfloat16)

    all_bins = asked[...].reshape(n_col, LANES).astype(jnp.float32)
    here = (local == iota((LANES, slots), 0)).astype(jnp.float32)
    bin_of = jnp.sum(jnp.where(owned, dot(all_bins, here), 0.0), axis=0, keepdims=True).astype(jnp.int32)
    n_bins = bin_scale.shape[1]
    square = (n_bins, n_bins)
    scales = jnp.sum(
        jnp.where(iota(square, 0) == iota(square, 1), jnp.broadcast_to(bin_scale[...], square), 0.0),
        axis=1,
        keepdims=True,
    )
    scale_of = jnp.sum(jnp.where(bin_of == iota((n_bins, slots), 0), scales, 0.0), axis=0, keepdims=True)
    of_bucket = (lax.div(iota((n_row, slots), 1), cap) == iota((n_row, slots), 0)).astype(jnp.float32)
    live = lax.rem(iota((1, slots), 1), cap).astype(jnp.float32) < dot(counts[...].astype(jnp.float32), of_bucket)
    weights[...] = pair_up(jnp.where(live, scale_of, 0.0), slots // 2)

    store_place.wait()
    lane_at = iota((groups, LANES), 1)

    def gather_thirds(group, count):
        peers = [col_peer(group, i) for i in range(n_z)]
        for peer in peers[:count]:
            wait_bytes(got.at[pl.ds(peer * REQ, 3)], answer_in.at[peer])
        joined = []
        for peer in peers:
            a, b, d = (
                pltpu.roll(got[peer * REQ + v].astype(jnp.float32), thirds * (v + 1), 1) for v in range(3)
            )
            joined.append(jnp.where(lane_at < thirds, a, jnp.where(lane_at < 2 * thirds, b, d)))
        for peer, tile in zip(peers, joined):
            got[peer * REQ + 3] = tile.astype(jnp.bfloat16)

    gather_thirds(0, n_z - 1)

    @pl.loop(1, n_y)
    def _(g):
        gather_thirds(g, n_z)

    low = iota((CASES, LANES), 1) < LANES // 2

    def term(slot):
        panel = got[place_s[0, slot]]
        both = jnp.dot(panel, packed[slot], preferred_element_type=jnp.float32)
        return both[:CASES], both[CASES:]

    def bucket(d):
        pairs = []
        for pair in range(cap // 2):
            a0, a1 = term(d * cap + 2 * pair)
            b0, b1 = term(d * cap + 2 * pair + 1)
            both = jnp.where(low, a0, b1) + pltpu.roll(jnp.where(low, b0, a1), LANES // 2, 1)
            pairs.append(both * weights[pl.ds(d * (cap // 2) + pair, 1), :])
        return pairs

    def store(dest, at, pairs):
        for pair, value in enumerate(pairs):
            dest[at, pair * CASES : (pair + 1) * CASES, :] = value

    def send(peers, summed):
        for peer, pairs in zip(peers, summed):
            store(terms, peer, pairs)
            to_row(terms.at[peer], summands.at[row], term_sem, term_in.at[row], peer).start()

    together = min(4, n_row)

    @pl.loop(0, n_row // together - 1)
    def _(g):
        peers = [row_peer(g * together + i) for i in range(together)]
        send(peers, [bucket(d) for d in peers])

    peers = [row_peer(n_row - together + i) for i in range(together - 1)]
    summed = [bucket(d) for d in peers + [row]]
    send(peers, summed[:-1])
    store(summands, row, summed[-1])

    def add(r, sums):
        for pair in range(cap // 2):
            value = summands[r, pair * CASES : (pair + 1) * CASES, :]
            to = got_cols[r, pair : pair + 1, :]
            sums = tuple(s + jnp.where(to == a, value, 0.0) for a, s in enumerate(sums))
        return sums

    @pl.loop(0, n_row - 1)
    def _(t):
        peer = row_peer(t)
        wait_bytes(got_cols.at[peer], cols_in.at[peer])

    def arrive(peers, sums):
        for peer in peers:
            wait_bytes(summands.at[peer], term_in.at[peer])
        for peer in peers:
            sums = add(peer, sums)
        return sums

    def group_of(g):
        return [row_peer(n_row - 1 - g * together - i) for i in range(together)]

    sums = add(row, (jnp.zeros((CASES, LANES), jnp.float32),) * AG_DEV)
    sums = arrive(group_of(0)[1:], sums)
    sums = lax.fori_loop(1, n_row // together, lambda g, sums: arrive(group_of(g), sums), sums)
    for a, s in enumerate(sums):
        s = s + pltpu.roll(s, LANES // 2, 1)
        folded[a * CASES : (a + 1) * CASES, :] = jnp.where(low, s, pltpu.roll(s, CASES - 1, 0))
    for j in range(CASES // 2):
        coarse[:, j * LANES : (j + 1) * LANES] = folded[pl.ds(2 * j, AG_DEV, stride=CASES), :]

    wait_bytes(ask.at[pl.ds(0, n_col - 1)], ask_sem)
    wait_bytes(cols.at[pl.ds(0, n_row - 1)], cols_sem)
    wait_bytes(answer.at[pl.ds(0, n_col - 1)], answer_sem)
    wait_bytes(terms.at[pl.ds(0, n_row - 1)], term_sem)


def shards(n_row, n_col, residual, bins, bin_scale, blocks, block_row, block_col, counts):
    slots, entries = blocks.shape
    fine_dev, width = residual.shape
    cap = slots // n_row
    dofs = width // CASES
    aggregate = entries // dofs
    tiles = entries // LANES
    f32, bf16, i32 = jnp.float32, jnp.bfloat16, jnp.int32
    vmem = pl.BlockSpec(memory_space=pltpu.VMEM)
    hbm = pl.BlockSpec(memory_space=pltpu.HBM)
    dma = pltpu.SemaphoreType.DMA
    out = pl.pallas_call(
        functools.partial(kernel, n_row, n_col),
        out_shape=jax.ShapeDtypeStruct((AG_DEV, CASES * aggregate), f32),
        in_specs=[hbm] * 7,
        out_specs=vmem,
        scratch_shapes=[
            pltpu.VMEM((1, slots), i32),
            pltpu.VMEM((1, slots), i32),
            pltpu.VMEM((1, fine_dev), i32),
            pltpu.VMEM((1, n_row), i32),
            pltpu.VMEM((1, bin_scale.shape[0]), f32),
            pltpu.VMEM((1, LANES), i32),
            pltpu.VMEM((fine_dev, width), bf16),
            pltpu.VMEM((slots, entries), bf16),
            pltpu.VMEM(((slots + 1) * (tiles + 1), LANES), f32),
            pltpu.VMEM((slots, LANES, LANES), bf16),
            pltpu.VMEM((fine_dev, 2 * CASES, LANES), f32),
            pltpu.VMEM((n_col, 1, LANES), i32),
            pltpu.VMEM((n_col, 1, LANES), i32),
            pltpu.VMEM((1, LANES), i32),
            pltpu.SMEM((1, LANES), i32),
            pltpu.VMEM((n_col, 3, 2 * CASES, LANES), bf16),
            pltpu.VMEM((n_col * REQ, 2 * CASES, LANES), bf16),
            pltpu.VMEM((n_row, cap // 2 * CASES, LANES), f32),
            pltpu.VMEM((n_row, cap // 2 * CASES, LANES), f32),
            pltpu.VMEM((n_row, cap // 2, LANES), i32),
            pltpu.VMEM((n_row, cap // 2, LANES), i32),
            pltpu.VMEM((slots // 2, LANES), f32),
            pltpu.VMEM(((AG_DEV + 1) * CASES, LANES), f32),
            dma((7,)),
        ]
        + [dma, dma, dma((n_col,)), dma, dma((n_col,))]
        + [dma, dma((n_row,)), dma, dma((n_row,))],
        compiler_params=pltpu.CompilerParams(
            collective_id=0, has_side_effects=True, vmem_limit_bytes=32 * 1024 * 1024
        ),
    )(
        *(
            pltpu.with_memory_space_constraint(a, pltpu.HBM)
            for a in (
                residual,
                blocks,
                block_row.reshape(1, -1),
                block_col.reshape(1, -1),
                bins.reshape(1, -1),
                counts.reshape(1, -1),
                bin_scale.reshape(1, -1),
            )
        )
    )
    return out[None]


def solution(mesh):
    both = P(("row", "col"))
    rows = P(("row", "col"), None)
    return jax.shard_map(
        functools.partial(shards, mesh.shape["row"], mesh.shape["col"]),
        mesh=mesh,
        in_specs=(rows, both, P(), rows, both, both, both),
        out_specs=P("col", "row", None),
        check_vma=False,
    )
```
